32 devices in a mesh: slab: 4 (over y, x), box: 8 (over z, core).
Axes of the slice: x: 2, y: 2, z: 4, core: 2. Of those that a mesh axis runs over, the one named last changes fastest.
Arguments:
- currents: bfloat16 [256, 128, 128], P(('slab', 'box')), may hold values from -6 to 6
- aggregate: bfloat16 [2, 512, 128], replicated, may hold values from -0.5 to 0.5
- disaggregate: bfloat16 [128, 2, 512], replicated, may hold values from -0.1875 to 0.1875
- trans_table: float32 [316, 2, 512], replicated, may hold values from -3 to 3
- trans_src: int32 [256, 4], P('slab'), may hold values from 0 to 63
- trans_kind: int32 [256, 4], P('slab'), may hold values from 0 to 315
- near_blocks: bfloat16 [27, 128, 128], replicated, may hold values from -0.109375 to 0.109375
- near_src: int32 [256, 27], P(('slab', 'box')), may hold values from 0 to 23
- near_kind: int32 [256, 27], P(('slab', 'box')), may hold values from 0 to 26
Outputs:
- field: float32 [256, 128, 128], P(('slab', 'box'))
The draws below stay inside these ranges and needn't reach their ends.
All inputs are finite; a program needn't handle non-finite values.
Results may differ from the reference program's by a relative error of at most 0.0035.
Values may be sent and summed in bfloat16 or wider, within the bound.
A program may use at most 64 MiB of HBM per device.

```python
import jax
import jax.numpy as jnp
from jax import lax

UNK = 128
DIRS = 512
EXC = 128
BOX_DEV = 8
TL = 4
NL = 27
NKIND = 316
NEARK = 27
SLAB_BOXES = 64
NBOX = 256
N_SLAB = 4
N_BOX = 8


def place_ends(values, key, least, largest):
    spot = [jax.random.randint(jax.random.fold_in(key, axis), (), 0, length) for axis, length in enumerate(values.shape)]
    widest = values.shape.index(max(values.shape))
    next_to = spot[:widest] + [(spot[widest] + 1) % values.shape[widest]] + spot[widest + 1:]
    return values.at[tuple(spot)].set(least).at[tuple(next_to)].set(largest)


def levels(rng, dims, shards, low, high):
    def one(position, blocks):
        draws = jax.random.uniform(jax.random.fold_in(jax.random.fold_in(rng, 6), position), (blocks,), jnp.float32, low / len(shards), high / len(shards))
        return jnp.repeat(jnp.exp(draws), dims[position] // blocks).reshape((-1,) + (1,) * (len(dims) - position - 1))

    level = one(*shards[0])
    for cut in shards[1:]:
        level = level * one(*cut)
    return level


def bell_draw(key, dims, scale, bound, shards=(), kind=jnp.bfloat16):
    array = scale * jax.random.normal(key, dims, jnp.float32)
    if shards:
        array = array * levels(key, dims, shards, -0.22, 0.18)
    return jnp.clip(array, -bound, bound).astype(kind)


def setup_inputs(seed: int = 0) -> dict:
    keys = jax.random.split(jax.random.key(seed), 10)
    return {
        "currents": bell_draw(keys[0], (NBOX, UNK, EXC), 1.0, 6.0, ((0, 32),)),
        "aggregate": bell_draw(keys[1], (2, DIRS, UNK), UNK ** -0.5, 0.5),
        "disaggregate": bell_draw(keys[2], (UNK, 2, DIRS), (2 * DIRS) ** -0.5, 0.1875),
        "trans_table": bell_draw(keys[3], (NKIND, 2, DIRS), 0.5, 3.0, (), jnp.float32),
        "trans_src": place_ends(jax.random.randint(keys[4], (NBOX, TL), 0, SLAB_BOXES), jax.random.fold_in(keys[4], 1), 0, SLAB_BOXES - 1).astype(jnp.int32),
        "trans_kind": place_ends(jax.random.randint(keys[5], (NBOX, TL), 0, NKIND), jax.random.fold_in(keys[5], 1), 0, NKIND - 1).astype(jnp.int32),
        "near_blocks": bell_draw(keys[6], (NEARK, UNK, UNK), (UNK * NL) ** -0.5, 0.109375),
        "near_src": place_ends(jax.random.randint(keys[7], (NBOX, NL), 0, 3 * BOX_DEV), jax.random.fold_in(keys[7], 1), 0, (3 * BOX_DEV) - 1).astype(jnp.int32),
        "near_kind": place_ends(jax.random.randint(keys[8], (NBOX, NL), 0, NEARK), jax.random.fold_in(keys[8], 1), 0, NEARK - 1).astype(jnp.int32),
    }


def reference(currents, aggregate, disaggregate, trans_table, trans_src, trans_kind, near_blocks, near_src, near_kind):
    slab_boxes = BOX_DEV * N_BOX
    by_slab = currents.reshape(N_SLAB, slab_boxes, UNK, EXC)
    src_slab = trans_src.reshape(N_SLAB, slab_boxes, TL)
    kind_slab = trans_kind.reshape(N_SLAB, slab_boxes, TL)
    agg_wide = aggregate.astype(jnp.float32)
    dis_wide = disaggregate.astype(jnp.float32)

    def slab_far(packed):
        block, sources, kinds = packed
        pattern = jnp.einsum('cdu,bue->bcde', agg_wide, block.astype(jnp.float32)).astype(jnp.bfloat16)
        real_part = jnp.zeros((slab_boxes, DIRS, EXC), jnp.float32)
        imag_part = jnp.zeros((slab_boxes, DIRS, EXC), jnp.float32)
        for entry in range(TL):
            source = pattern[sources[:, entry]].astype(jnp.float32)
            coeffs = trans_table[kinds[:, entry]]
            coef_real = coeffs[:, 0, :, None]
            coef_imag = coeffs[:, 1, :, None]
            real_part = real_part + (coef_real * source[:, 0] - coef_imag * source[:, 1])
            imag_part = imag_part + (coef_real * source[:, 1] + coef_imag * source[:, 0])
        incoming = jnp.stack([real_part, imag_part], 1).astype(jnp.bfloat16)
        return jnp.einsum('ucd,bcde->bue', dis_wide, incoming.astype(jnp.float32))

    far = lax.map(slab_far, (by_slab, src_slab, kind_slab)).reshape(NBOX, UNK, EXC)

    grouped = currents.reshape(N_SLAB, N_BOX, BOX_DEV, UNK, EXC)
    nothing = jnp.zeros_like(grouped[:1])
    below_slab = jnp.concatenate([nothing, grouped[:-1]], 0)
    above_slab = jnp.concatenate([grouped[1:], nothing], 0)
    candidates = jnp.concatenate([below_slab, grouped, above_slab], 2)
    groups = N_SLAB * N_BOX
    candidates = candidates.reshape(groups, 3 * BOX_DEV, UNK, EXC)
    group_ids = jnp.arange(groups, dtype=jnp.int32)[:, None]

    def add_entry(running, columns):
        src_col, kind_col = columns
        sources = candidates[group_ids, src_col.reshape(groups, BOX_DEV)].reshape(NBOX, UNK, EXC)
        blocks = near_blocks[kind_col]
        running = running + jnp.einsum('buv,bve->bue', blocks.astype(jnp.float32), sources.astype(jnp.float32))
        return running, None

    near, unused = lax.scan(add_entry, jnp.zeros((NBOX, UNK, EXC), jnp.float32), (near_src.T, near_kind.T))
    return near + far
```

```python
import functools

import jax
import jax.numpy as jnp
from jax import lax
from jax.experimental import pallas as pl
from jax.experimental.pallas import tpu as pltpu
from jax.sharding import PartitionSpec as P

MESH = pl.DeviceIdType.MESH
CHUNKS = 2


def spread(total, parts):
    return [total * i // parts for i in range(parts + 1)]


def kernel(
    n_slab,
    n_box,
    trans_src,
    trans_kind,
    near_src,
    near_kind,
    currents,
    aggregate,
    disaggregate,
    trans_table,
    near_blocks,
    out,
    gathered,
    cand,
    agg,
    dis,
    dis_wide,
    table,
    blocks,
    weights,
    operators,
    load_sem,
    halo_send,
    halo_recv,
    own_send,
    line_send,
    line_recv,
    pair_send,
    pair_recv,
):
    slab = lax.axis_index("slab")
    box = lax.axis_index("box")
    place = box // 2
    core = box % 2
    chips = n_box // 2
    n_own, unk, exc = currents.shape
    per = n_own // CHUNKS
    dirs = agg.shape[1]
    n_trans = trans_src.shape[0]
    n_near = near_src.shape[1]

    def peer(slab_step, box_id):
        return (slab + slab_step, box_id)

    pair_id = place * 2 + (1 - core)
    neighbours = [
        (place > 0, peer(0, box - 2)),
        (place < chips - 1, peer(0, box + 2)),
        (None, peer(0, pair_id)),
        (slab > 0, peer(-1, box)),
        (slab < n_slab - 1, peer(1, box)),
    ]

    def when(cond):
        return (lambda f: f()) if cond is None else pl.when(cond)

    own = pl.ds(box * n_own, n_own)
    loads = [
        pltpu.make_async_copy(currents, gathered.at[own], load_sem.at[0]),
        pltpu.make_async_copy(currents, cand.at[pl.ds(n_own, n_own)], load_sem.at[1]),
        pltpu.make_async_copy(disaggregate, dis, load_sem.at[2]),
        pltpu.make_async_copy(trans_table, table, load_sem.at[3]),
        pltpu.make_async_copy(aggregate, agg, load_sem.at[4]),
        pltpu.make_async_copy(near_blocks, blocks, load_sem.at[5]),
    ]
    for load in loads:
        load.start()

    barrier = pltpu.get_barrier_semaphore()
    for cond, target in neighbours:
        @when(cond)
        def _():
            pl.semaphore_signal(barrier, inc=1, device_id=target, device_id_type=MESH)
    met = (
        1
        + (place > 0).astype(jnp.int32)
        + (place < chips - 1).astype(jnp.int32)
        + (slab > 0).astype(jnp.int32)
        + (slab < n_slab - 1).astype(jnp.int32)
    )
    pl.semaphore_wait(barrier, met)

    def part(origin, lane, chunk):
        return gathered.at[pl.ds((origin * 2 + lane) * n_own + chunk * per, per)]

    def line_copy(origin, chunk, target, send):
        return pltpu.make_async_remote_copy(
            src_ref=part(origin, core, chunk),
            dst_ref=part(origin, core, chunk),
            send_sem=send,
            recv_sem=line_recv.at[origin, chunk],
            device_id=peer(0, target),
            device_id_type=MESH,
        )

    def pair_copy(origin, lane, chunk):
        return pltpu.make_async_remote_copy(
            src_ref=part(origin, lane, chunk),
            dst_ref=part(origin, lane, chunk),
            send_sem=pair_send.at[origin, chunk],
            recv_sem=pair_recv.at[origin, chunk],
            device_id=peer(0, pair_id),
            device_id_type=MESH,
        )

    def halo_copy(side):
        return pltpu.make_async_remote_copy(
            src_ref=cand.at[pl.ds(n_own, n_own)],
            dst_ref=cand.at[pl.ds(2 * n_own * side, n_own)],
            send_sem=halo_send.at[side],
            recv_sem=halo_recv.at[side],
            device_id=peer(1 - 2 * side, box),
            device_id_type=MESH,
        )

    loads[0].wait()
    for chunk in range(CHUNKS):
        @pl.when(place < chips - 1)
        def _():
            line_copy(place, chunk, box + 2, own_send.at[0, chunk]).start()

        @pl.when(place > 0)
        def _():
            line_copy(place, chunk, box - 2, own_send.at[1, chunk]).start()

    loads[1].wait()

    @pl.when(slab < n_slab - 1)
    def _():
        halo_copy(0).start()

    @pl.when(slab > 0)
    def _():
        halo_copy(1).start()

    for chunk in range(CHUNKS):
        pair_copy(place, core, chunk).start()

    @pl.when(slab == 0)
    def _():
        cand[pl.ds(0, n_own)] = jnp.zeros((n_own, unk, exc), cand.dtype)

    @pl.when(slab == n_slab - 1)
    def _():
        cand[pl.ds(2 * n_own, n_own)] = jnp.zeros((n_own, unk, exc), cand.dtype)

    loads[2].wait()
    dis_wide[0] = dis[:, 0, :].astype(jnp.float32)
    dis_wide[1] = dis[:, 1, :].astype(jnp.float32)
    loads[3].wait()
    loads[4].wait()

    rows = 32

    def operator_unit(b, carry):
        for entry in range(n_trans):
            coef = table[trans_kind[entry, box * n_own + b]]
            coef_real = coef[0:1]
            coef_imag = coef[1:2]
            for r in range(0, unk, rows):
                dis_real = dis_wide[0, r : r + rows]
                dis_imag = dis_wide[1, r : r + rows]
                at = pl.ds(entry * unk + r, rows)
                weights[at, 0:dirs] = (dis_real * coef_real + dis_imag * coef_imag).astype(
                    jnp.bfloat16
                )
                weights[at, dirs : 2 * dirs] = (
                    dis_imag * coef_real - dis_real * coef_imag
                ).astype(jnp.bfloat16)
        product = jnp.dot(
            weights[...],
            agg[...].reshape(2 * dirs, unk),
            preferred_element_type=jnp.float32,
        )
        high = product.astype(jnp.bfloat16)
        low = (product - high.astype(jnp.float32)).astype(jnp.bfloat16)
        for entry in range(n_trans):
            columns = pl.ds(entry * unk, unk)
            operators[b, 0:unk, columns] = high[entry * unk : (entry + 1) * unk]
            operators[b, unk : 2 * unk, columns] = low[entry * unk : (entry + 1) * unk]
        return carry

    def near_unit(b, carry):
        lhs = jnp.concatenate([blocks[near_kind[b, i]] for i in range(n_near)], axis=1)
        rhs = jnp.concatenate([cand[near_src[b, i]] for i in range(n_near)], axis=0)
        out[b] = jnp.dot(lhs, rhs, preferred_element_type=jnp.float32)
        return carry

    def far_unit(b, carry):
        rhs = jnp.concatenate(
            [gathered[trans_src[i, box * n_own + b]] for i in range(n_trans)], axis=0
        )
        both = jnp.dot(operators[b], rhs, preferred_element_type=jnp.float32)
        out[b] = out[b] + (both[0:unk] + both[unk:])
        return carry

    def forward(step, chunk):
        from_low = place - step
        from_high = place + step

        @pl.when(from_low >= 0)
        def _():
            line_copy(from_low, chunk, box, own_send.at[0, chunk]).wait_recv()

            @pl.when(place < chips - 1)
            def _():
                line_copy(from_low, chunk, box + 2, line_send.at[from_low, chunk]).start()

            pair_copy(from_low, core, chunk).start()

        @pl.when(from_high < chips)
        def _():
            line_copy(from_high, chunk, box, own_send.at[1, chunk]).wait_recv()

            @pl.when(place > 0)
            def _():
                line_copy(from_high, chunk, box - 2, line_send.at[from_high, chunk]).start()

            pair_copy(from_high, core, chunk).start()

    def halo_wait():
        @pl.when(slab > 0)
        def _():
            halo_copy(0).wait_recv()

        @pl.when(slab < n_slab - 1)
        def _():
            halo_copy(1).wait_recv()

    events = [(step, chunk) for step in range(1, chips) for chunk in range(CHUNKS)]
    cuts = spread(2 * n_own, len(events))
    halo_done = False
    for number, (step, chunk) in enumerate(events):
        lo, hi = cuts[number], cuts[number + 1]
        if lo < min(hi, n_own):
            lax.fori_loop(lo, min(hi, n_own), operator_unit, 0)
        if hi > n_own:
            if not halo_done:
                halo_wait()
                loads[5].wait()
                halo_done = True
            lax.fori_loop(max(lo, n_own) - n_own, hi - n_own, near_unit, 0)
        forward(step, chunk)

    for origin in range(chips):
        for chunk in range(CHUNKS):
            pair_copy(origin, 1 - core, chunk).wait_recv()

    lax.fori_loop(0, n_own, far_unit, 0)

    for origin in range(chips):
        for chunk in range(CHUNKS):
            pair_copy(origin, core, chunk).wait_send()

            @pl.when(((origin < place) & (place < chips - 1)) | ((origin > place) & (place > 0)))
            def _():
                line_copy(origin, chunk, box, line_send.at[origin, chunk]).wait_send()

    for chunk in range(CHUNKS):
        @pl.when(place < chips - 1)
        def _():
            line_copy(place, chunk, box + 2, own_send.at[0, chunk]).wait_send()

        @pl.when(place > 0)
        def _():
            line_copy(place, chunk, box - 2, own_send.at[1, chunk]).wait_send()

    @pl.when(slab < n_slab - 1)
    def _():
        halo_copy(0).wait_send()

    @pl.when(slab > 0)
    def _():
        halo_copy(1).wait_send()


def on_device(
    n_slab,
    n_box,
    currents,
    aggregate,
    disaggregate,
    trans_table,
    trans_src,
    trans_kind,
    near_blocks,
    near_src,
    near_kind,
):
    n_own, unk, exc = currents.shape
    dirs = aggregate.shape[1]
    n_trans = trans_src.shape[1]
    chips = n_box // 2
    smem = pl.BlockSpec(memory_space=pltpu.SMEM)
    anywhere = pl.BlockSpec(memory_space=pl.ANY)
    dma = pltpu.SemaphoreType.DMA
    return pl.pallas_call(
        functools.partial(kernel, n_slab, n_box),
        out_shape=jax.ShapeDtypeStruct((n_own, unk, exc), jnp.float32),
        in_specs=[smem] * 4 + [anywhere] * 5,
        out_specs=pl.BlockSpec(memory_space=pltpu.VMEM),
        scratch_shapes=[
            pltpu.VMEM((n_box * n_own, unk, exc), jnp.bfloat16),
            pltpu.VMEM((3 * n_own, unk, exc), jnp.bfloat16),
            pltpu.VMEM(aggregate.shape, jnp.bfloat16),
            pltpu.VMEM(disaggregate.shape, jnp.bfloat16),
            pltpu.VMEM((2, unk, dirs), jnp.float32),
            pltpu.VMEM(trans_table.shape, jnp.float32),
            pltpu.VMEM(near_blocks.shape, jnp.bfloat16),
            pltpu.VMEM((n_trans * unk, 2 * dirs), jnp.bfloat16),
            pltpu.VMEM((n_own, 2 * unk, n_trans * unk), jnp.bfloat16),
            dma((6,)),
            dma((2,)),
            dma((2,)),
            dma((2, CHUNKS)),
            dma((chips, CHUNKS)),
            dma((chips, CHUNKS)),
            dma((chips, CHUNKS)),
            dma((chips, CHUNKS)),
        ],
        compiler_params=pltpu.CompilerParams(
            collective_id=0, has_side_effects=True, vmem_limit_bytes=60 * 2**20
        ),
    )(
        trans_src.T,
        trans_kind.T,
        near_src,
        near_kind,
        currents,
        aggregate,
        disaggregate,
        trans_table,
        near_blocks,
    )


def solution(mesh):
    placed = (
        P(("slab", "box"), None, None),
        P(),
        P(),
        P(),
        P("slab", None),
        P("slab", None),
        P(),
        P(("slab", "box"), None),
        P(("slab", "box"), None),
    )
    return jax.shard_map(
        functools.partial(on_device, mesh.shape["slab"], mesh.shape["box"]),
        mesh=mesh,
        in_specs=placed,
        out_specs=P(("slab", "box"), None, None),
        check_vma=False,
    )
```

```python
import functools

import jax
import jax.numpy as jnp
from jax import lax
from jax.experimental import pallas as pl
from jax.experimental.pallas import tpu as pltpu
from jax.sharding import PartitionSpec as P

MESH = pl.DeviceIdType.MESH
CHUNKS = 2


def spread(total, parts):
    return [total * i // parts for i in range(parts + 1)]


def kernel(
    n_slab,
    n_box,
    trans_src,
    trans_kind,
    near_src,
    near_kind,
    currents,
    aggregate,
    disaggregate,
    trans_table,
    near_blocks,
    out,
    gathered,
    cand,
    agg,
    dis,
    dis_wide,
    table,
    blocks,
    weights,
    operators,
    load_sem,
    halo_send,
    halo_recv,
    own_send,
    line_send,
    line_recv,
    pair_send,
    pair_recv,
):
    slab = lax.axis_index("slab")
    box = lax.axis_index("box")
    place = box // 2
    core = box % 2
    chips = n_box // 2
    n_own, unk, exc = currents.shape
    first = n_own * 3 // 4
    starts = (0, first)
    sizes = (first, n_own - first)
    dirs = agg.shape[1]
    n_trans = trans_src.shape[0]
    n_near = near_src.shape[1]

    def peer(slab_step, box_id):
        return (slab + slab_step, box_id)

    pair_id = place * 2 + (1 - core)
    neighbours = [
        (place > 0, peer(0, box - 2)),
        (place < chips - 1, peer(0, box + 2)),
        (None, peer(0, pair_id)),
        (slab > 0, peer(-1, box)),
        (slab < n_slab - 1, peer(1, box)),
    ]

    def when(cond):
        return (lambda f: f()) if cond is None else pl.when(cond)

    own = pl.ds(box * n_own, n_own)
    loads = [
        pltpu.make_async_copy(currents, gathered.at[own], load_sem.at[0]),
        pltpu.make_async_copy(currents, cand.at[pl.ds(n_own, n_own)], load_sem.at[1]),
        pltpu.make_async_copy(disaggregate, dis, load_sem.at[2]),
        pltpu.make_async_copy(trans_table, table, load_sem.at[3]),
        pltpu.make_async_copy(aggregate, agg, load_sem.at[4]),
        pltpu.make_async_copy(near_blocks, blocks, load_sem.at[5]),
    ]
    for load in loads[:2]:
        load.start()

    barrier = pltpu.get_barrier_semaphore()
    for cond, target in neighbours:
        @when(cond)
        def _():
            pl.semaphore_signal(barrier, inc=1, device_id=target, device_id_type=MESH)
    met = (
        1
        + (place > 0).astype(jnp.int32)
        + (place < chips - 1).astype(jnp.int32)
        + (slab > 0).astype(jnp.int32)
        + (slab < n_slab - 1).astype(jnp.int32)
    )
    pl.semaphore_wait(barrier, met)

    def part(origin, lane, chunk):
        return gathered.at[pl.ds((origin * 2 + lane) * n_own + starts[chunk], sizes[chunk])]

    def line_copy(origin, chunk, target, send):
        return pltpu.make_async_remote_copy(
            src_ref=part(origin, core, chunk),
            dst_ref=part(origin, core, chunk),
            send_sem=send,
            recv_sem=line_recv.at[origin, chunk],
            device_id=peer(0, target),
            device_id_type=MESH,
        )

    def pair_copy(origin, lane, chunk):
        return pltpu.make_async_remote_copy(
            src_ref=part(origin, lane, chunk),
            dst_ref=part(origin, lane, chunk),
            send_sem=pair_send.at[origin, chunk],
            recv_sem=pair_recv.at[origin, chunk],
            device_id=peer(0, pair_id),
            device_id_type=MESH,
        )

    def halo_copy(side):
        return pltpu.make_async_remote_copy(
            src_ref=cand.at[pl.ds(n_own, n_own)],
            dst_ref=cand.at[pl.ds(2 * n_own * side, n_own)],
            send_sem=halo_send.at[side],
            recv_sem=halo_recv.at[side],
            device_id=peer(1 - 2 * side, box),
            device_id_type=MESH,
        )

    loads[0].wait()
    for chunk in range(CHUNKS):
        @pl.when(place < chips - 1)
        def _():
            line_copy(place, chunk, box + 2, own_send.at[0, chunk]).start()

        @pl.when(place > 0)
        def _():
            line_copy(place, chunk, box - 2, own_send.at[1, chunk]).start()

    for load in loads[2:]:
        load.start()
    loads[1].wait()

    @pl.when(slab < n_slab - 1)
    def _():
        halo_copy(0).start()

    @pl.when(slab > 0)
    def _():
        halo_copy(1).start()

    for chunk in range(CHUNKS):
        pair_copy(place, core, chunk).start()

    @pl.when(slab == 0)
    def _():
        cand[pl.ds(0, n_own)] = jnp.zeros((n_own, unk, exc), cand.dtype)

    @pl.when(slab == n_slab - 1)
    def _():
        cand[pl.ds(2 * n_own, n_own)] = jnp.zeros((n_own, unk, exc), cand.dtype)

    loads[2].wait()
    dis_wide[0] = dis[:, 0, :].astype(jnp.float32)
    dis_wide[1] = dis[:, 1, :].astype(jnp.float32)
    loads[3].wait()
    loads[4].wait()

    rows = 32

    def operator_unit(b, carry):
        for entry in range(n_trans):
            coef = table[trans_kind[entry, box * n_own + b]]
            coef_real = coef[0:1]
            coef_imag = coef[1:2]
            for r in range(0, unk, rows):
                dis_real = dis_wide[0, r : r + rows]
                dis_imag = dis_wide[1, r : r + rows]
                at = pl.ds(entry * unk + r, rows)
                weights[at, 0:dirs] = (dis_real * coef_real + dis_imag * coef_imag).astype(
                    jnp.bfloat16
                )
                weights[at, dirs : 2 * dirs] = (
                    dis_imag * coef_real - dis_real * coef_imag
                ).astype(jnp.bfloat16)
        product = jnp.dot(
            weights[...],
            agg[...].reshape(2 * dirs, unk),
            preferred_element_type=jnp.float32,
        )
        high = product.astype(jnp.bfloat16)
        low = (product - high.astype(jnp.float32)).astype(jnp.bfloat16)
        for entry in range(n_trans):
            columns = pl.ds(entry * unk, unk)
            operators[b, 0:unk, columns] = high[entry * unk : (entry + 1) * unk]
            operators[b, unk : 2 * unk, columns] = low[entry * unk : (entry + 1) * unk]
        return carry

    def near_unit(b, carry):
        lhs = jnp.concatenate([blocks[near_kind[b, i]] for i in range(n_near)], axis=1)
        rhs = jnp.concatenate([cand[near_src[b, i]] for i in range(n_near)], axis=0)
        out[b] = jnp.dot(lhs, rhs, preferred_element_type=jnp.float32)
        return carry

    def far_unit(b, carry):
        rhs = jnp.concatenate(
            [gathered[trans_src[i, box * n_own + b]] for i in range(n_trans)], axis=0
        )
        both = jnp.dot(operators[b], rhs, preferred_element_type=jnp.float32)
        out[b] = out[b] + (both[0:unk] + both[unk:])
        return carry

    def forward(step, chunk):
        from_low = place - step
        from_high = place + step

        @pl.when(from_low >= 0)
        def _():
            line_copy(from_low, chunk, box, own_send.at[0, chunk]).wait_recv()

            @pl.when(place < chips - 1)
            def _():
                line_copy(from_low, chunk, box + 2, line_send.at[from_low, chunk]).start()

            pair_copy(from_low, core, chunk).start()

        @pl.when(from_high < chips)
        def _():
            line_copy(from_high, chunk, box, own_send.at[1, chunk]).wait_recv()

            @pl.when(place > 0)
            def _():
                line_copy(from_high, chunk, box - 2, line_send.at[from_high, chunk]).start()

            pair_copy(from_high, core, chunk).start()

    def halo_wait():
        @pl.when(slab > 0)
        def _():
            halo_copy(0).wait_recv()

        @pl.when(slab < n_slab - 1)
        def _():
            halo_copy(1).wait_recv()

    events = [(step, chunk) for step in range(1, chips) for chunk in range(CHUNKS)]
    cuts = spread(2 * n_own, len(events))
    halo_done = False
    for number, (step, chunk) in enumerate(events):
        lo, hi = cuts[number], cuts[number + 1]
        if lo < min(hi, n_own):
            lax.fori_loop(lo, min(hi, n_own), operator_unit, 0)
        if hi > n_own:
            if not halo_done:
                halo_wait()
                loads[5].wait()
                halo_done = True
            lax.fori_loop(max(lo, n_own) - n_own, hi - n_own, near_unit, 0)
        forward(step, chunk)

    for origin in range(chips):
        for chunk in range(CHUNKS):
            pair_copy(origin, 1 - core, chunk).wait_recv()

    for b in range(n_own):
        far_unit(b, 0)

    for origin in range(chips):
        for chunk in range(CHUNKS):
            pair_copy(origin, core, chunk).wait_send()

            @pl.when(((origin < place) & (place < chips - 1)) | ((origin > place) & (place > 0)))
            def _():
                line_copy(origin, chunk, box, line_send.at[origin, chunk]).wait_send()

    for chunk in range(CHUNKS):
        @pl.when(place < chips - 1)
        def _():
            line_copy(place, chunk, box + 2, own_send.at[0, chunk]).wait_send()

        @pl.when(place > 0)
        def _():
            line_copy(place, chunk, box - 2, own_send.at[1, chunk]).wait_send()

    @pl.when(slab < n_slab - 1)
    def _():
        halo_copy(0).wait_send()

    @pl.when(slab > 0)
    def _():
        halo_copy(1).wait_send()


def on_device(
    n_slab,
    n_box,
    currents,
    aggregate,
    disaggregate,
    trans_table,
    trans_src,
    trans_kind,
    near_blocks,
    near_src,
    near_kind,
):
    n_own, unk, exc = currents.shape
    dirs = aggregate.shape[1]
    n_trans = trans_src.shape[1]
    chips = n_box // 2
    smem = pl.BlockSpec(memory_space=pltpu.SMEM)
    anywhere = pl.BlockSpec(memory_space=pl.ANY)
    dma = pltpu.SemaphoreType.DMA
    return pl.pallas_call(
        functools.partial(kernel, n_slab, n_box),
        out_shape=jax.ShapeDtypeStruct((n_own, unk, exc), jnp.float32),
        in_specs=[smem] * 4 + [anywhere] * 5,
        out_specs=pl.BlockSpec(memory_space=pltpu.VMEM),
        scratch_shapes=[
            pltpu.VMEM((n_box * n_own, unk, exc), jnp.bfloat16),
            pltpu.VMEM((3 * n_own, unk, exc), jnp.bfloat16),
            pltpu.VMEM(aggregate.shape, jnp.bfloat16),
            pltpu.VMEM(disaggregate.shape, jnp.bfloat16),
            pltpu.VMEM((2, unk, dirs), jnp.float32),
            pltpu.VMEM(trans_table.shape, jnp.float32),
            pltpu.VMEM(near_blocks.shape, jnp.bfloat16),
            pltpu.VMEM((n_trans * unk, 2 * dirs), jnp.bfloat16),
            pltpu.VMEM((n_own, 2 * unk, n_trans * unk), jnp.bfloat16),
            dma((6,)),
            dma((2,)),
            dma((2,)),
            dma((2, CHUNKS)),
            dma((chips, CHUNKS)),
            dma((chips, CHUNKS)),
            dma((chips, CHUNKS)),
            dma((chips, CHUNKS)),
        ],
        compiler_params=pltpu.CompilerParams(
            collective_id=0, has_side_effects=True, vmem_limit_bytes=60 * 2**20
        ),
    )(
        trans_src.T,
        trans_kind.T,
        near_src,
        near_kind,
        currents,
        aggregate,
        disaggregate,
        trans_table,
        near_blocks,
    )


def solution(mesh):
    placed = (
        P(("slab", "box"), None, None),
        P(),
        P(),
        P(),
        P("slab", None),
        P("slab", None),
        P(),
        P(("slab", "box"), None),
        P(("slab", "box"), None),
    )
    return jax.shard_map(
        functools.partial(on_device, mesh.shape["slab"], mesh.shape["box"]),
        mesh=mesh,
        in_specs=placed,
        out_specs=P(("slab", "box"), None, None),
        check_vma=False,
    )
```

```python
import functools

import jax
import jax.numpy as jnp
from jax import lax
from jax.experimental import pallas as pl
from jax.experimental.pallas import tpu as pltpu
from jax.sharding import PartitionSpec as P

MESH = pl.DeviceIdType.MESH
CHUNKS = 2


def spread(total, parts):
    return [total * i // parts for i in range(parts + 1)]


def kernel(
    n_slab,
    n_box,
    trans_src,
    trans_kind,
    near_src,
    near_kind,
    currents,
    aggregate,
    disaggregate,
    trans_table,
    near_blocks,
    out,
    gathered,
    cand,
    agg,
    dis,
    dis_wide,
    table,
    blocks,
    total,
    weights,
    operators,
    load_sem,
    store_sem,
    halo_send,
    halo_recv,
    own_send,
    line_send,
    line_recv,
    pair_send,
    pair_recv,
):
    slab = lax.axis_index("slab")
    box = lax.axis_index("box")
    place = box // 2
    core = box % 2
    chips = n_box // 2
    n_own, unk, exc = currents.shape
    first = n_own * 3 // 4
    starts = (0, first)
    sizes = (first, n_own - first)
    dirs = agg.shape[1]
    n_trans = trans_src.shape[0]
    n_near = near_src.shape[1]

    def peer(slab_step, box_id):
        return (slab + slab_step, box_id)

    pair_id = place * 2 + (1 - core)
    neighbours = [
        (place > 0, peer(0, box - 2)),
        (place < chips - 1, peer(0, box + 2)),
        (None, peer(0, pair_id)),
        (slab > 0, peer(-1, box)),
        (slab < n_slab - 1, peer(1, box)),
    ]

    def when(cond):
        return (lambda f: f()) if cond is None else pl.when(cond)

    own = pl.ds(box * n_own, n_own)
    loads = [
        pltpu.make_async_copy(currents, gathered.at[own], load_sem.at[0]),
        pltpu.make_async_copy(currents, cand.at[pl.ds(n_own, n_own)], load_sem.at[1]),
        pltpu.make_async_copy(disaggregate, dis, load_sem.at[2]),
        pltpu.make_async_copy(trans_table, table, load_sem.at[3]),
        pltpu.make_async_copy(aggregate, agg, load_sem.at[4]),
        pltpu.make_async_copy(near_blocks, blocks, load_sem.at[5]),
    ]
    for load in loads[:2]:
        load.start()

    barrier = pltpu.get_barrier_semaphore()
    for cond, target in neighbours:
        @when(cond)
        def _():
            pl.semaphore_signal(barrier, inc=1, device_id=target, device_id_type=MESH)
    met = (
        1
        + (place > 0).astype(jnp.int32)
        + (place < chips - 1).astype(jnp.int32)
        + (slab > 0).astype(jnp.int32)
        + (slab < n_slab - 1).astype(jnp.int32)
    )
    pl.semaphore_wait(barrier, met)

    def part(origin, lane, chunk):
        return gathered.at[pl.ds((origin * 2 + lane) * n_own + starts[chunk], sizes[chunk])]

    def line_copy(origin, chunk, target, send):
        return pltpu.make_async_remote_copy(
            src_ref=part(origin, core, chunk),
            dst_ref=part(origin, core, chunk),
            send_sem=send,
            recv_sem=line_recv.at[origin, chunk],
            device_id=peer(0, target),
            device_id_type=MESH,
        )

    def pair_copy(origin, lane, chunk):
        return pltpu.make_async_remote_copy(
            src_ref=part(origin, lane, chunk),
            dst_ref=part(origin, lane, chunk),
            send_sem=pair_send.at[origin, chunk],
            recv_sem=pair_recv.at[origin, chunk],
            device_id=peer(0, pair_id),
            device_id_type=MESH,
        )

    def halo_copy(side):
        return pltpu.make_async_remote_copy(
            src_ref=cand.at[pl.ds(n_own, n_own)],
            dst_ref=cand.at[pl.ds(2 * n_own * side, n_own)],
            send_sem=halo_send.at[side],
            recv_sem=halo_recv.at[side],
            device_id=peer(1 - 2 * side, box),
            device_id_type=MESH,
        )

    loads[0].wait()
    for chunk in range(CHUNKS):
        @pl.when(place < chips - 1)
        def _():
            line_copy(place, chunk, box + 2, own_send.at[0, chunk]).start()

        @pl.when(place > 0)
        def _():
            line_copy(place, chunk, box - 2, own_send.at[1, chunk]).start()

    for load in loads[2:]:
        load.start()
    loads[1].wait()

    @pl.when(slab < n_slab - 1)
    def _():
        halo_copy(0).start()

    @pl.when(slab > 0)
    def _():
        halo_copy(1).start()

    for chunk in range(CHUNKS):
        pair_copy(place, core, chunk).start()

    @pl.when(slab == 0)
    def _():
        cand[pl.ds(0, n_own)] = jnp.zeros((n_own, unk, exc), cand.dtype)

    @pl.when(slab == n_slab - 1)
    def _():
        cand[pl.ds(2 * n_own, n_own)] = jnp.zeros((n_own, unk, exc), cand.dtype)

    loads[2].wait()
    dis_wide[0] = dis[:, 0, :].astype(jnp.float32)
    dis_wide[1] = dis[:, 1, :].astype(jnp.float32)
    loads[3].wait()
    loads[4].wait()

    rows = 32

    def operator_unit(b, carry):
        for entry in range(n_trans):
            coef = table[trans_kind[entry, box * n_own + b]]
            coef_real = coef[0:1]
            coef_imag = coef[1:2]
            for r in range(0, unk, rows):
                dis_real = dis_wide[0, r : r + rows]
                dis_imag = dis_wide[1, r : r + rows]
                at = pl.ds(entry * unk + r, rows)
                weights[at, 0:dirs] = (dis_real * coef_real + dis_imag * coef_imag).astype(
                    jnp.bfloat16
                )
                weights[at, dirs : 2 * dirs] = (
                    dis_imag * coef_real - dis_real * coef_imag
                ).astype(jnp.bfloat16)
        product = jnp.dot(
            weights[...],
            agg[...].reshape(2 * dirs, unk),
            preferred_element_type=jnp.float32,
        )
        high = product.astype(jnp.bfloat16)
        low = (product - high.astype(jnp.float32)).astype(jnp.bfloat16)
        for entry in range(n_trans):
            columns = pl.ds(entry * unk, unk)
            operators[b, 0:unk, columns] = high[entry * unk : (entry + 1) * unk]
            operators[b, unk : 2 * unk, columns] = low[entry * unk : (entry + 1) * unk]
        return carry

    def near_unit(b, carry):
        lhs = jnp.concatenate([blocks[near_kind[b, i]] for i in range(n_near)], axis=1)
        rhs = jnp.concatenate([cand[near_src[b, i]] for i in range(n_near)], axis=0)
        total[b] = jnp.dot(lhs, rhs, preferred_element_type=jnp.float32)
        return carry

    def far_unit(b, carry):
        rhs = jnp.concatenate(
            [gathered[trans_src[i, box * n_own + b]] for i in range(n_trans)], axis=0
        )
        both = jnp.dot(operators[b], rhs, preferred_element_type=jnp.float32)
        total[b] = total[b] + (both[0:unk] + both[unk:])
        return carry

    def forward(step, chunk):
        from_low = place - step
        from_high = place + step

        @pl.when(from_low >= 0)
        def _():
            line_copy(from_low, chunk, box, own_send.at[0, chunk]).wait_recv()

            @pl.when(place < chips - 1)
            def _():
                line_copy(from_low, chunk, box + 2, line_send.at[from_low, chunk]).start()

            pair_copy(from_low, core, chunk).start()

        @pl.when(from_high < chips)
        def _():
            line_copy(from_high, chunk, box, own_send.at[1, chunk]).wait_recv()

            @pl.when(place > 0)
            def _():
                line_copy(from_high, chunk, box - 2, line_send.at[from_high, chunk]).start()

            pair_copy(from_high, core, chunk).start()

    def halo_wait():
        @pl.when(slab > 0)
        def _():
            halo_copy(0).wait_recv()

        @pl.when(slab < n_slab - 1)
        def _():
            halo_copy(1).wait_recv()

    events = [(step, chunk) for step in range(1, chips) for chunk in range(CHUNKS)]
    cuts = spread(2 * n_own, len(events))
    halo_done = False
    for number, (step, chunk) in enumerate(events):
        lo, hi = cuts[number], cuts[number + 1]
        if lo < min(hi, n_own):
            lax.fori_loop(lo, min(hi, n_own), operator_unit, 0)
        if hi > n_own:
            if not halo_done:
                halo_wait()
                loads[5].wait()
                halo_done = True
            lax.fori_loop(max(lo, n_own) - n_own, hi - n_own, near_unit, 0)
        forward(step, chunk)

    for origin in range(chips):
        for chunk in range(CHUNKS):
            pair_copy(origin, 1 - core, chunk).wait_recv()

    for b in range(n_own):
        far_unit(b, 0)
        pltpu.make_async_copy(total.at[b], out.at[b], store_sem.at[b]).start()

    for origin in range(chips):
        for chunk in range(CHUNKS):
            pair_copy(origin, core, chunk).wait_send()

            @pl.when(((origin < place) & (place < chips - 1)) | ((origin > place) & (place > 0)))
            def _():
                line_copy(origin, chunk, box, line_send.at[origin, chunk]).wait_send()

    for chunk in range(CHUNKS):
        @pl.when(place < chips - 1)
        def _():
            line_copy(place, chunk, box + 2, own_send.at[0, chunk]).wait_send()

        @pl.when(place > 0)
        def _():
            line_copy(place, chunk, box - 2, own_send.at[1, chunk]).wait_send()

    @pl.when(slab < n_slab - 1)
    def _():
        halo_copy(0).wait_send()

    @pl.when(slab > 0)
    def _():
        halo_copy(1).wait_send()

    for b in range(n_own):
        pltpu.make_async_copy(total.at[b], out.at[b], store_sem.at[b]).wait()


def hand_on(source, out, sem):
    copies = [
        pltpu.make_async_copy(source.at[b], out.at[b], sem.at[b])
        for b in range(source.shape[0])
    ]
    for copy in copies:
        copy.start()
    for copy in copies:
        copy.wait()


def on_device(
    n_slab,
    n_box,
    currents,
    aggregate,
    disaggregate,
    trans_table,
    trans_src,
    trans_kind,
    near_blocks,
    near_src,
    near_kind,
):
    n_own, unk, exc = currents.shape
    dirs = aggregate.shape[1]
    n_trans = trans_src.shape[1]
    chips = n_box // 2
    smem = pl.BlockSpec(memory_space=pltpu.SMEM)
    anywhere = pl.BlockSpec(memory_space=pl.ANY)
    dma = pltpu.SemaphoreType.DMA
    field = pl.pallas_call(
        functools.partial(kernel, n_slab, n_box),
        out_shape=jax.ShapeDtypeStruct((n_own, unk, exc), jnp.float32),
        in_specs=[smem] * 4 + [anywhere] * 5,
        out_specs=anywhere,
        scratch_shapes=[
            pltpu.VMEM((n_box * n_own, unk, exc), jnp.bfloat16),
            pltpu.VMEM((3 * n_own, unk, exc), jnp.bfloat16),
            pltpu.VMEM(aggregate.shape, jnp.bfloat16),
            pltpu.VMEM(disaggregate.shape, jnp.bfloat16),
            pltpu.VMEM((2, unk, dirs), jnp.float32),
            pltpu.VMEM(trans_table.shape, jnp.float32),
            pltpu.VMEM(near_blocks.shape, jnp.bfloat16),
            pltpu.VMEM((n_own, unk, exc), jnp.float32),
            pltpu.VMEM((n_trans * unk, 2 * dirs), jnp.bfloat16),
            pltpu.VMEM((n_own, 2 * unk, n_trans * unk), jnp.bfloat16),
            dma((6,)),
            dma((n_own,)),
            dma((2,)),
            dma((2,)),
            dma((2, CHUNKS)),
            dma((chips, CHUNKS)),
            dma((chips, CHUNKS)),
            dma((chips, CHUNKS)),
            dma((chips, CHUNKS)),
        ],
        compiler_params=pltpu.CompilerParams(
            collective_id=0, has_side_effects=True, vmem_limit_bytes=60 * 2**20
        ),
    )(
        trans_src.T,
        trans_kind.T,
        near_src,
        near_kind,
        currents,
        aggregate,
        disaggregate,
        trans_table,
        near_blocks,
    )
    return pl.pallas_call(
        hand_on,
        out_shape=jax.ShapeDtypeStruct(field.shape, field.dtype),
        in_specs=[anywhere],
        out_specs=anywhere,
        scratch_shapes=[dma((n_own,))],
    )(field)


def solution(mesh):
    placed = (
        P(("slab", "box"), None, None),
        P(),
        P(),
        P(),
        P("slab", None),
        P("slab", None),
        P(),
        P(("slab", "box"), None),
        P(("slab", "box"), None),
    )
    return jax.shard_map(
        functools.partial(on_device, mesh.shape["slab"], mesh.shape["box"]),
        mesh=mesh,
        in_specs=placed,
        out_specs=P(("slab", "box"), None, None),
        check_vma=False,
    )
```

```python
import functools

import jax
import jax.numpy as jnp
from jax import lax
from jax.experimental import pallas as pl
from jax.experimental.pallas import tpu as pltpu
from jax.sharding import PartitionSpec as P

MESH = pl.DeviceIdType.MESH
CHUNKS = 2


def spread(total, parts):
    return [total * i // parts for i in range(parts + 1)]


def kernel(
    n_slab,
    n_box,
    trans_src,
    trans_kind,
    near_src,
    near_kind,
    currents,
    aggregate,
    disaggregate,
    trans_table,
    near_blocks,
    out,
    gathered,
    cand,
    agg,
    dis,
    dis_wide,
    table,
    blocks,
    total,
    weights,
    operators,
    load_sem,
    store_sem,
    halo_send,
    halo_recv,
    own_send,
    line_send,
    line_recv,
    pair_send,
    pair_recv,
):
    slab = lax.axis_index("slab")
    box = lax.axis_index("box")
    place = box // 2
    core = box % 2
    chips = n_box // 2
    n_own, unk, exc = currents.shape
    first = n_own * 3 // 4
    starts = (0, first)
    sizes = (first, n_own - first)
    dirs = agg.shape[1]
    n_trans = trans_src.shape[0]
    n_near = near_src.shape[1]

    def peer(slab_step, box_id):
        return (slab + slab_step, box_id)

    pair_id = place * 2 + (1 - core)
    neighbours = [
        (place > 0, peer(0, box - 2)),
        (place < chips - 1, peer(0, box + 2)),
        (None, peer(0, pair_id)),
        (slab > 0, peer(-1, box)),
        (slab < n_slab - 1, peer(1, box)),
    ]

    def when(cond):
        return (lambda f: f()) if cond is None else pl.when(cond)

    own = pl.ds(box * n_own, n_own)
    loads = [
        pltpu.make_async_copy(currents, gathered.at[own], load_sem.at[0]),
        pltpu.make_async_copy(currents, cand.at[pl.ds(n_own, n_own)], load_sem.at[1]),
        pltpu.make_async_copy(disaggregate, dis, load_sem.at[2]),
        pltpu.make_async_copy(trans_table, table, load_sem.at[3]),
        pltpu.make_async_copy(aggregate, agg, load_sem.at[4]),
        pltpu.make_async_copy(near_blocks, blocks, load_sem.at[5]),
    ]
    for load in loads[:2]:
        load.start()

    barrier = pltpu.get_barrier_semaphore()
    for cond, target in neighbours:
        @when(cond)
        def _():
            pl.semaphore_signal(barrier, inc=1, device_id=target, device_id_type=MESH)
    met = (
        1
        + (place > 0).astype(jnp.int32)
        + (place < chips - 1).astype(jnp.int32)
        + (slab > 0).astype(jnp.int32)
        + (slab < n_slab - 1).astype(jnp.int32)
    )
    pl.semaphore_wait(barrier, met)

    def part(origin, lane, chunk):
        return gathered.at[pl.ds((origin * 2 + lane) * n_own + starts[chunk], sizes[chunk])]

    def line_copy(origin, chunk, target, send):
        return pltpu.make_async_remote_copy(
            src_ref=part(origin, core, chunk),
            dst_ref=part(origin, core, chunk),
            send_sem=send,
            recv_sem=line_recv.at[origin, chunk],
            device_id=peer(0, target),
            device_id_type=MESH,
        )

    def pair_copy(origin, lane, chunk):
        return pltpu.make_async_remote_copy(
            src_ref=part(origin, lane, chunk),
            dst_ref=part(origin, lane, chunk),
            send_sem=pair_send.at[origin, chunk],
            recv_sem=pair_recv.at[origin, chunk],
            device_id=peer(0, pair_id),
            device_id_type=MESH,
        )

    def halo_copy(side):
        return pltpu.make_async_remote_copy(
            src_ref=cand.at[pl.ds(n_own, n_own)],
            dst_ref=cand.at[pl.ds(2 * n_own * side, n_own)],
            send_sem=halo_send.at[side],
            recv_sem=halo_recv.at[side],
            device_id=peer(1 - 2 * side, box),
            device_id_type=MESH,
        )

    loads[0].wait()
    for chunk in range(CHUNKS):
        @pl.when(place < chips - 1)
        def _():
            line_copy(place, chunk, box + 2, own_send.at[0, chunk]).start()

        @pl.when(place > 0)
        def _():
            line_copy(place, chunk, box - 2, own_send.at[1, chunk]).start()

    for load in loads[2:]:
        load.start()
    loads[1].wait()

    @pl.when(slab < n_slab - 1)
    def _():
        halo_copy(0).start()

    @pl.when(slab > 0)
    def _():
        halo_copy(1).start()

    for chunk in range(CHUNKS):
        pair_copy(place, core, chunk).start()

    @pl.when(slab == 0)
    def _():
        cand[pl.ds(0, n_own)] = jnp.zeros((n_own, unk, exc), cand.dtype)

    @pl.when(slab == n_slab - 1)
    def _():
        cand[pl.ds(2 * n_own, n_own)] = jnp.zeros((n_own, unk, exc), cand.dtype)

    loads[2].wait()
    dis_wide[0] = dis[:, 0, :].astype(jnp.float32)
    dis_wide[1] = dis[:, 1, :].astype(jnp.float32)
    loads[3].wait()
    loads[4].wait()

    rows = 32

    def operator_unit(b, carry):
        for entry in range(n_trans):
            coef = table[trans_kind[entry, box * n_own + b]]
            coef_real = coef[0:1]
            coef_imag = coef[1:2]
            for r in range(0, unk, rows):
                dis_real = dis_wide[0, r : r + rows]
                dis_imag = dis_wide[1, r : r + rows]
                at = pl.ds(entry * unk + r, rows)
                weights[at, 0:dirs] = (dis_real * coef_real + dis_imag * coef_imag).astype(
                    jnp.bfloat16
                )
                weights[at, dirs : 2 * dirs] = (
                    dis_imag * coef_real - dis_real * coef_imag
                ).astype(jnp.bfloat16)
        product = jnp.dot(
            weights[...],
            agg[...].reshape(2 * dirs, unk),
            preferred_element_type=jnp.float32,
        )
        high = product.astype(jnp.bfloat16)
        low = (product - high.astype(jnp.float32)).astype(jnp.bfloat16)
        for entry in range(n_trans):
            columns = pl.ds(entry * unk, unk)
            operators[b, 0:unk, columns] = high[entry * unk : (entry + 1) * unk]
            operators[b, unk : 2 * unk, columns] = low[entry * unk : (entry + 1) * unk]
        return carry

    def near_unit(b, carry):
        lhs = jnp.concatenate([blocks[near_kind[b, i]] for i in range(n_near)], axis=1)
        rhs = jnp.concatenate([cand[near_src[b, i]] for i in range(n_near)], axis=0)
        total[b] = jnp.dot(lhs, rhs, preferred_element_type=jnp.float32)
        return carry

    def far_unit(b, carry):
        rhs = jnp.concatenate(
            [gathered[trans_src[i, box * n_own + b]] for i in range(n_trans)], axis=0
        )
        both = jnp.dot(operators[b], rhs, preferred_element_type=jnp.float32)
        total[b] = total[b] + (both[0:unk] + both[unk:])
        return carry

    def forward(step, chunk):
        from_low = place - step
        from_high = place + step

        @pl.when(from_low >= 0)
        def _():
            line_copy(from_low, chunk, box, own_send.at[0, chunk]).wait_recv()

            @pl.when(place < chips - 1)
            def _():
                line_copy(from_low, chunk, box + 2, line_send.at[from_low, chunk]).start()

            pair_copy(from_low, core, chunk).start()

        @pl.when(from_high < chips)
        def _():
            line_copy(from_high, chunk, box, own_send.at[1, chunk]).wait_recv()

            @pl.when(place > 0)
            def _():
                line_copy(from_high, chunk, box - 2, line_send.at[from_high, chunk]).start()

            pair_copy(from_high, core, chunk).start()

    def halo_wait():
        @pl.when(slab > 0)
        def _():
            halo_copy(0).wait_recv()

        @pl.when(slab < n_slab - 1)
        def _():
            halo_copy(1).wait_recv()

    events = [(step, chunk) for step in range(1, chips) for chunk in range(CHUNKS)]
    cuts = spread(2 * n_own, len(events))
    halo_done = False
    for number, (step, chunk) in enumerate(events):
        lo, hi = cuts[number], cuts[number + 1]
        if lo < min(hi, n_own):
            lax.fori_loop(lo, min(hi, n_own), operator_unit, 0)
        if hi > n_own:
            if not halo_done:
                halo_wait()
                loads[5].wait()
                halo_done = True
            lax.fori_loop(max(lo, n_own) - n_own, hi - n_own, near_unit, 0)
        forward(step, chunk)

    for origin in range(chips):
        for chunk in range(CHUNKS):
            pair_copy(origin, 1 - core, chunk).wait_recv()

    for b in range(n_own):
        far_unit(b, 0)
        pltpu.make_async_copy(total.at[b], out.at[b], store_sem.at[b]).start()

    for origin in range(chips):
        for chunk in range(CHUNKS):
            pair_copy(origin, core, chunk).wait_send()

            @pl.when(((origin < place) & (place < chips - 1)) | ((origin > place) & (place > 0)))
            def _():
                line_copy(origin, chunk, box, line_send.at[origin, chunk]).wait_send()

    for chunk in range(CHUNKS):
        @pl.when(place < chips - 1)
        def _():
            line_copy(place, chunk, box + 2, own_send.at[0, chunk]).wait_send()

        @pl.when(place > 0)
        def _():
            line_copy(place, chunk, box - 2, own_send.at[1, chunk]).wait_send()

    @pl.when(slab < n_slab - 1)
    def _():
        halo_copy(0).wait_send()

    @pl.when(slab > 0)
    def _():
        halo_copy(1).wait_send()

    for b in range(n_own):
        pltpu.make_async_copy(total.at[b], out.at[b], store_sem.at[b]).wait()


def hand_on(source, out, held, load_sem, store_sem):
    count = source.shape[0]
    loads = [pltpu.make_async_copy(source.at[b], held.at[b], load_sem.at[b]) for b in range(count)]
    stores = [pltpu.make_async_copy(held.at[b], out.at[b], store_sem.at[b]) for b in range(count)]
    for load in loads:
        load.start()
    for load, store in zip(loads, stores):
        load.wait()
        store.start()
    for store in stores:
        store.wait()


def on_device(
    n_slab,
    n_box,
    currents,
    aggregate,
    disaggregate,
    trans_table,
    trans_src,
    trans_kind,
    near_blocks,
    near_src,
    near_kind,
):
    n_own, unk, exc = currents.shape
    dirs = aggregate.shape[1]
    n_trans = trans_src.shape[1]
    chips = n_box // 2
    smem = pl.BlockSpec(memory_space=pltpu.SMEM)
    anywhere = pl.BlockSpec(memory_space=pl.ANY)
    dma = pltpu.SemaphoreType.DMA
    field = pl.pallas_call(
        functools.partial(kernel, n_slab, n_box),
        out_shape=jax.ShapeDtypeStruct((n_own, unk, exc), jnp.float32),
        in_specs=[smem] * 4 + [anywhere] * 5,
        out_specs=anywhere,
        scratch_shapes=[
            pltpu.VMEM((n_box * n_own, unk, exc), jnp.bfloat16),
            pltpu.VMEM((3 * n_own, unk, exc), jnp.bfloat16),
            pltpu.VMEM(aggregate.shape, jnp.bfloat16),
            pltpu.VMEM(disaggregate.shape, jnp.bfloat16),
            pltpu.VMEM((2, unk, dirs), jnp.float32),
            pltpu.VMEM(trans_table.shape, jnp.float32),
            pltpu.VMEM(near_blocks.shape, jnp.bfloat16),
            pltpu.VMEM((n_own, unk, exc), jnp.float32),
            pltpu.VMEM((n_trans * unk, 2 * dirs), jnp.bfloat16),
            pltpu.VMEM((n_own, 2 * unk, n_trans * unk), jnp.bfloat16),
            dma((6,)),
            dma((n_own,)),
            dma((2,)),
            dma((2,)),
            dma((2, CHUNKS)),
            dma((chips, CHUNKS)),
            dma((chips, CHUNKS)),
            dma((chips, CHUNKS)),
            dma((chips, CHUNKS)),
        ],
        compiler_params=pltpu.CompilerParams(
            collective_id=0, has_side_effects=True, vmem_limit_bytes=60 * 2**20
        ),
    )(
        trans_src.T,
        trans_kind.T,
        near_src,
        near_kind,
        currents,
        aggregate,
        disaggregate,
        trans_table,
        near_blocks,
    )
    return pl.pallas_call(
        hand_on,
        out_shape=jax.ShapeDtypeStruct(field.shape, field.dtype),
        in_specs=[anywhere],
        out_specs=anywhere,
        scratch_shapes=[pltpu.VMEM(field.shape, field.dtype), dma((n_own,)), dma((n_own,))],
    )(field)


def solution(mesh):
    placed = (
        P(("slab", "box"), None, None),
        P(),
        P(),
        P(),
        P("slab", None),
        P("slab", None),
        P(),
        P(("slab", "box"), None),
        P(("slab", "box"), None),
    )
    return jax.shard_map(
        functools.partial(on_device, mesh.shape["slab"], mesh.shape["box"]),
        mesh=mesh,
        in_specs=placed,
        out_specs=P(("slab", "box"), None, None),
        check_vma=False,
    )
```
